32 devices in a mesh: img: 4 (over y, x), txt: 8 (over z, core).
Axes of the slice: x: 2, y: 2, z: 4, core: 2. Of those that a mesh axis runs over, the one named last changes fastest.
Arguments:
- img_emb: bfloat16 [160, 1152], P(('img', 'txt')), may hold values from -6 to 6
- txt_emb: bfloat16 [160, 1152], P(('img', 'txt')), may hold values from -6 to 6
- match: int32 [160], P(('img', 'txt')), may hold values from 0 to 159, each once
- log_temp: float32 [1], replicated, may hold values from 1.6 to 2.6
- bias: float32 [1], replicated, may hold values from -4 to -2
Outputs:
- grad_img: float32 [160, 1152], P(('img', 'txt'))
- grad_txt: float32 [160, 1152], P(('img', 'txt'))
- loss: float32 [1], replicated
- grad_log_temp: float32 [1], replicated
- grad_bias: float32 [1], replicated
The draws below stay inside these ranges and needn't reach their ends.
Inputs may be any that keep to these rules, and one draw needn't show every extreme that they name: match is a permutation of the text rows.
All inputs are finite; a program needn't handle non-finite values.
Results may differ from the reference program's by a relative error of at most 0.0042.
Values may be sent and summed in bfloat16 or wider, within the bound.
A program may use at most 64 MiB of HBM per device.

```python
import jax
import jax.numpy as jnp
from jax import lax

D = 1152
ROWS_DEV = 5
BATCH = 160
N_IMG = 4
N_TXT = 8


def block_levels(rng, shape, split, least, largest):
    loudness = 1.0
    for position, parts in split:
        draws = jax.random.uniform(jax.random.fold_in(jax.random.fold_in(rng, 6), position), (parts,), jnp.float32, least / len(split), largest / len(split))
        loudness = loudness * jnp.repeat(jnp.exp(draws), shape[position] // parts).reshape((-1,) + (1,) * (len(shape) - 1 - position))
    return loudness


def noise(own_key, dims, scale, limit, cuts=(), held_as=jnp.bfloat16):
    level = block_levels(own_key, dims, cuts, -0.22, 0.18) if cuts else 1.0
    drawn = jax.random.normal(own_key, dims, jnp.float32) * scale * level
    return jnp.minimum(jnp.maximum(drawn, -limit), limit).astype(held_as)


def setup_inputs(seed: int = 0) -> dict:
    arg_keys = jax.random.split(jax.random.key(seed), 6)
    return {
        "img_emb": noise(arg_keys[0], (BATCH, D), 1.0, 6.0, ((0, 32),)),
        "txt_emb": noise(arg_keys[1], (BATCH, D), 1.0, 6.0, ((0, 32),)),
        "match": jax.random.permutation(arg_keys[2], BATCH).astype(jnp.int32),
        "log_temp": jnp.clip(jax.random.uniform(arg_keys[3], (1,), jnp.float32, 1.6, 2.6), 1.6, 2.6),
        "bias": jnp.clip(jax.random.uniform(arg_keys[4], (1,), jnp.float32, -4.0, -2.0), -4.0, -2.0),
    }


def unit_rows(values):
    wide = values.astype(jnp.float32)
    length = jnp.sqrt(lax.optimization_barrier(jnp.sum(wide * wide, axis=-1, keepdims=True)) + 1e-06)
    return (wide / length, length)

def reference(img_emb, txt_emb, match, log_temp, bias):
    img_unit, img_norm = unit_rows(img_emb)
    txt_unit, txt_norm = unit_rows(txt_emb)
    img_cast = img_unit.astype(jnp.bfloat16)
    txt_cast = txt_unit.astype(jnp.bfloat16)
    temper = jnp.exp(log_temp[0])
    offset = bias[0]
    block_rows = ROWS_DEV * N_TXT
    img_blocks = img_cast.reshape(N_IMG, block_rows, D)
    match_blocks = match.reshape(N_IMG, block_rows)
    columns = jnp.arange(BATCH, dtype=jnp.int32)

    def step(carry, inputs):
        txt_acc, sums = carry
        rows_cast, rows_match = inputs
        products = lax.dot_general(rows_cast, txt_cast, (((1,), (1,)), ((), ())), preferred_element_type=jnp.float32)
        label_sign = jnp.where(rows_match[:, None] == columns[None, :], 1.0, -1.0).astype(jnp.float32)
        scaled = temper * products
        logits = scaled + offset
        slopes = -label_sign * jax.nn.sigmoid(-label_sign * logits)
        partial_value = jnp.stack([jnp.sum(jax.nn.softplus(-label_sign * logits)), jnp.sum(slopes), jnp.sum(slopes * scaled)])
        weighted = (temper * slopes).astype(jnp.bfloat16)
        img_term = jnp.dot(weighted, txt_cast, preferred_element_type=jnp.float32)
        txt_acc = txt_acc + lax.dot_general(weighted, rows_cast, (((0,), (0,)), ((), ())), preferred_element_type=jnp.float32)
        return ((txt_acc, sums + partial_value), img_term)
    start = (jnp.zeros((BATCH, D), jnp.float32), jnp.zeros((3,), jnp.float32))
    (grad_txt_unit, totals), img_terms = lax.scan(step, start, (img_blocks, match_blocks))
    grad_img_unit = img_terms.reshape(BATCH, D)
    grad_img = (grad_img_unit - img_unit * lax.optimization_barrier(jnp.sum(img_unit * grad_img_unit, axis=-1, keepdims=True))) / img_norm
    grad_txt = (grad_txt_unit - txt_unit * lax.optimization_barrier(jnp.sum(txt_unit * grad_txt_unit, axis=-1, keepdims=True))) / txt_norm
    pair_count = jnp.float32(BATCH) * jnp.float32(BATCH)
    totals = totals / pair_count
    return (grad_img, grad_txt, totals[0:1], totals[2:3], totals[1:2])
```

```python
import functools

import jax
import jax.numpy as jnp
from jax import lax
from jax.experimental import pallas as pl
from jax.experimental.pallas import tpu as pltpu
from jax.sharding import PartitionSpec as P

MESH = pl.DeviceIdType.MESH
PAD = 8
DIGIT = 64


def each(start, stop, body):
    if stop - start <= 32:
        for k in range(start, stop):
            body(k)
    else:
        lax.fori_loop(start, stop, lambda k, c: (body(k), c)[1], 0)


def kernel(
    n_img, n_txt,
    img_hbm, txt_hbm, match_ref, temp_ref, bias_ref,
    grad_img_ref, grad_txt_ref, loss_ref, dtemp_ref, dbias_ref,
    img_in, txt_in, img_all, txt_all, img_part, txt_part, img_back, txt_back, sums,
    in_sem, img_out, txt_out, txt_back_out, img_back_out, sums_out, img_sem, txt_sem, img_back_sem, txt_back_sem, sums_sem,
):
    rows, width = img_in.shape
    n_z = n_txt // 2
    n_plane = n_img * 2
    n_all = n_img * n_txt
    i = lax.axis_index("img")
    t = lax.axis_index("txt")
    z, core = t // 2, t % 2
    me = i * n_txt + t

    def plane(k, sign):
        return (
            lax.rem(i + sign * (k // 2) + n_img, n_img),
            z * 2 + lax.rem(core + k, 2),
        )

    def column(k, sign):
        return (i, lax.rem(z + sign * k + n_z, n_z) * 2 + core)

    def anyone(k):
        other = lax.rem(me + k, n_all)
        return (other // n_txt, lax.rem(other, n_txt))

    load_img = pltpu.make_async_copy(img_hbm, img_in, in_sem.at[0])
    load_txt = pltpu.make_async_copy(txt_hbm, txt_in, in_sem.at[1])
    load_img.start()
    load_txt.start()

    barrier = pltpu.get_barrier_semaphore()
    each(1, n_all, lambda k: pl.semaphore_signal(
        barrier, inc=1, device_id=anyone(k), device_id_type=MESH))

    def unit_rows(ref):
        wide = ref[...].astype(jnp.float32)
        norm = jnp.sqrt(jnp.sum(wide * wide, axis=-1, keepdims=True) + 1e-06)
        return wide / norm, norm

    load_img.wait()
    img_unit, img_norm = unit_rows(img_in)
    sub = lax.broadcasted_iota(jnp.int32, (PAD - rows, width), 0)
    lane = lax.broadcasted_iota(jnp.int32, (PAD - rows, width), 1)
    digits = jnp.zeros((PAD - rows, width), jnp.int32)
    for r in range(rows):
        m = match_ref[r]
        high = m // DIGIT
        digit = jnp.where(sub == 0, high, jnp.where(sub == 1, m - high * DIGIT, 0))
        digits = jnp.where(lane == r, digit, digits)
    img_all[0] = jnp.concatenate([img_unit, digits.astype(jnp.float32)], axis=0).astype(jnp.bfloat16)
    load_txt.wait()
    txt_unit, txt_norm = unit_rows(txt_in)
    txt_all[0] = jnp.concatenate(
        [txt_unit, jnp.zeros((PAD - rows, width), jnp.float32)], axis=0).astype(jnp.bfloat16)

    pl.semaphore_wait(barrier, n_all - 1)

    def img_copy(k):
        return pltpu.make_async_remote_copy(
            src_ref=img_all.at[0], dst_ref=img_all.at[k], send_sem=img_out.at[k],
            recv_sem=img_sem.at[k], device_id=plane(k, 1), device_id_type=MESH)

    def txt_copy(k):
        return pltpu.make_async_remote_copy(
            src_ref=txt_all.at[0], dst_ref=txt_all.at[k], send_sem=txt_out.at[k],
            recv_sem=txt_sem.at[k], device_id=column(k, 1), device_id_type=MESH)

    each(1, n_z, lambda k: txt_copy(k).start())
    each(1, n_plane, lambda k: img_copy(k).start())

    each(1, n_z, lambda k: txt_copy(k).wait_recv())
    each(1, n_plane, lambda k: img_copy(k).wait_recv())

    n_rows, n_cols = n_plane * PAD, n_z * PAD
    img_rows = img_all[...].astype(jnp.float32).reshape(n_rows, width).astype(jnp.bfloat16)
    txt_rows = txt_all[...].astype(jnp.float32).reshape(n_cols, width).astype(jnp.bfloat16)
    products = lax.dot_general(
        img_rows, txt_rows, (((1,), (1,)), ((), ())), preferred_element_type=jnp.float32)

    head = img_all[:, :, 0:128].astype(jnp.float32)
    whole = head[:, rows:rows + 1, :] * float(DIGIT) + head[:, rows + 1:rows + 2, :]
    spot = lax.broadcasted_iota(jnp.int32, (n_plane, PAD, 128), 1)
    at = lax.broadcasted_iota(jnp.int32, (n_plane, PAD, 128), 2)
    labels = jnp.sum(
        jnp.where(spot == at, jnp.broadcast_to(whole, (n_plane, PAD, 128)), 0.0),
        axis=-1, keepdims=True).reshape(n_rows, 1)

    row = lax.broadcasted_iota(jnp.int32, (n_rows, n_cols), 0)
    col = lax.broadcasted_iota(jnp.int32, (n_rows, n_cols), 1)
    slot = col // PAD
    place = lax.rem(z - slot + n_z, n_z) * 2 + core
    global_col = (i * n_txt + place) * rows + col % PAD
    valid = (row % PAD < rows) & (col % PAD < rows)
    sign = jnp.where(labels == global_col.astype(jnp.float32), 1.0, -1.0)

    temper = jnp.exp(jnp.full((1, 1), temp_ref[0], jnp.float32))
    scaled = temper * products
    margin = sign * (scaled + bias_ref[0])
    small = jnp.exp(-jnp.abs(margin))
    pair_loss = jnp.maximum(-margin, 0.0) + jnp.log1p(small)
    slopes = jnp.where(valid, -sign * jnp.where(margin >= 0.0, small, 1.0) / (1.0 + small), 0.0)
    pair_loss = jnp.where(valid, pair_loss, 0.0)

    def total(values):
        return jnp.sum(jnp.sum(values, axis=0, keepdims=True), axis=1, keepdims=True)

    lane = lax.broadcasted_iota(jnp.int32, (1, 128), 1)
    sums[0] = jnp.where(
        lane == 0, total(pair_loss),
        jnp.where(lane == 1, total(slopes * scaled), jnp.where(lane == 2, total(slopes), 0.0)))

    def sums_copy(k):
        return pltpu.make_async_remote_copy(
            src_ref=sums.at[0], dst_ref=sums.at[k], send_sem=sums_out.at[k],
            recv_sem=sums_sem.at[k], device_id=anyone(k), device_id_type=MESH)

    weighted = (temper * slopes).astype(jnp.bfloat16)
    txt_term = lax.dot_general(
        weighted, img_rows, (((0,), (0,)), ((), ())), preferred_element_type=jnp.float32)
    txt_part[...] = txt_term.reshape(n_z, PAD, width).astype(jnp.bfloat16)

    def txt_back_copy(k):
        return pltpu.make_async_remote_copy(
            src_ref=txt_part.at[k], dst_ref=txt_back.at[k], send_sem=txt_back_out.at[k],
            recv_sem=txt_back_sem.at[k], device_id=column(k, -1), device_id_type=MESH)

    each(1, n_z, lambda k: txt_back_copy(k).start())

    img_term = jnp.dot(weighted, txt_rows, preferred_element_type=jnp.float32)
    img_part[...] = img_term.reshape(n_plane, PAD, width).astype(jnp.bfloat16)

    def img_back_copy(k):
        return pltpu.make_async_remote_copy(
            src_ref=img_part.at[k], dst_ref=img_back.at[k], send_sem=img_back_out.at[k],
            recv_sem=img_back_sem.at[k], device_id=plane(k, -1), device_id_type=MESH)

    each(1, n_plane, lambda k: img_back_copy(k).start())
    each(1, n_all, lambda k: sums_copy(k).start())

    def unit_back(unit, norm, upstream):
        return (upstream - unit * jnp.sum(unit * upstream, axis=-1, keepdims=True)) / norm

    def gather_sum(own, back, n, copy):
        each(1, n, lambda k: copy(k).wait_recv())
        return (own + jnp.sum(back[1:].astype(jnp.float32), axis=0))[0:rows]

    grad_txt_unit = gather_sum(txt_term[0:PAD], txt_back, n_z, txt_back_copy)
    grad_txt_ref[...] = unit_back(txt_unit, txt_norm, grad_txt_unit)
    grad_img_unit = gather_sum(img_term[0:PAD], img_back, n_plane, img_back_copy)
    grad_img_ref[...] = unit_back(img_unit, img_norm, grad_img_unit)

    each(1, n_all, lambda k: sums_copy(k).wait_recv())
    batch = jnp.float32(rows * n_all)
    totals = jnp.sum(sums[...], axis=0) / (batch * batch)
    loss_ref[0] = jnp.sum(jnp.where(lane == 0, totals, 0.0))
    dtemp_ref[0] = jnp.sum(jnp.where(lane == 1, totals, 0.0))
    dbias_ref[0] = jnp.sum(jnp.where(lane == 2, totals, 0.0))

    each(1, n_z, lambda k: (txt_copy(k).wait_send(), txt_back_copy(k).wait_send()))
    each(1, n_plane, lambda k: (img_copy(k).wait_send(), img_back_copy(k).wait_send()))
    each(1, n_all, lambda k: sums_copy(k).wait_send())


def solution(mesh):
    n_img, n_txt = mesh.shape["img"], mesh.shape["txt"]
    n_z, n_plane, n_all = n_txt // 2, n_img * 2, n_img * n_txt

    def per_device(img_emb, txt_emb, match, log_temp, bias):
        rows, width = img_emb.shape
        smem = pl.BlockSpec(memory_space=pltpu.SMEM)
        vmem = pl.BlockSpec(memory_space=pltpu.VMEM)
        hbm = pl.BlockSpec(memory_space=pl.ANY)
        one = jax.ShapeDtypeStruct((1,), jnp.float32)
        grad = jax.ShapeDtypeStruct((rows, width), jnp.float32)
        dma = pltpu.SemaphoreType.DMA
        return pl.pallas_call(
            functools.partial(kernel, n_img, n_txt),
            out_shape=(grad, grad, one, one, one),
            in_specs=[hbm, hbm, smem, smem, smem],
            out_specs=(vmem, vmem, smem, smem, smem),
            scratch_shapes=[
                pltpu.VMEM((rows, width), jnp.bfloat16),
                pltpu.VMEM((rows, width), jnp.bfloat16),
                pltpu.VMEM((n_plane, PAD, width), jnp.bfloat16),
                pltpu.VMEM((n_z, PAD, width), jnp.bfloat16),
                pltpu.VMEM((n_plane, PAD, width), jnp.bfloat16),
                pltpu.VMEM((n_z, PAD, width), jnp.bfloat16),
                pltpu.VMEM((n_plane, PAD, width), jnp.bfloat16),
                pltpu.VMEM((n_z, PAD, width), jnp.bfloat16),
                pltpu.VMEM((n_all, 1, 128), jnp.float32),
                dma((2,)),
                dma((n_plane,)),
                dma((n_z,)),
                dma((n_z,)),
                dma((n_plane,)),
                dma((n_all,)),
                dma((n_plane,)),
                dma((n_z,)),
                dma((n_plane,)),
                dma((n_z,)),
                dma((n_all,)),
            ],
            compiler_params=pltpu.CompilerParams(
                collective_id=0, has_side_effects=True, vmem_limit_bytes=40 * 1024 * 1024),
        )(img_emb, txt_emb, match, log_temp, bias)

    split = P(("img", "txt"), None)
    return jax.shard_map(
        per_device,
        mesh=mesh,
        in_specs=(split, split, P(("img", "txt")), P(), P()),
        out_specs=(split, split, P(), P(), P()),
        check_vma=False,
    )
```

```python
import functools

import jax
import jax.numpy as jnp
from jax import lax
from jax.experimental import pallas as pl
from jax.experimental.pallas import tpu as pltpu
from jax.sharding import PartitionSpec as P

MESH = pl.DeviceIdType.MESH
PAD = 8
DIGIT = 64


def each(start, stop, body):
    if stop - start <= 32:
        for k in range(start, stop):
            body(k)
    else:
        lax.fori_loop(start, stop, lambda k, c: (body(k), c)[1], 0)


def kernel(
    n_img, n_txt,
    img_hbm, txt_hbm, match_hbm, temp_hbm, bias_hbm,
    grad_img_ref, grad_txt_ref, totals_ref,
    img_in, txt_in, match_ref, temp_ref, bias_ref, img_all, txt_all, img_part, txt_part, img_back, txt_back, sums, col_sums,
    in_sem, img_out, txt_out, img_back_out, txt_back_out, sums_out, col_sums_out,
    img_sem, txt_sem, img_back_sem, txt_back_sem, sums_sem, col_sums_sem,
):
    rows, width = img_in.shape
    n_z = n_txt // 2
    n_plane = n_img * 2
    i = lax.axis_index("img")
    t = lax.axis_index("txt")
    z, core = t // 2, t % 2

    def plane(k, sign):
        return (
            lax.rem(i + sign * (k // 2) + n_img, n_img),
            z * 2 + lax.rem(core + k, 2),
        )

    def column(k, sign):
        return (i, lax.rem(z + sign * k + n_z, n_z) * 2 + core)

    load_img = pltpu.make_async_copy(img_hbm, img_in, in_sem.at[0])
    load_txt = pltpu.make_async_copy(txt_hbm, txt_in, in_sem.at[1])
    small_loads = [
        pltpu.make_async_copy(match_hbm, match_ref, in_sem.at[2]),
        pltpu.make_async_copy(temp_hbm, temp_ref, in_sem.at[3]),
        pltpu.make_async_copy(bias_hbm, bias_ref, in_sem.at[4]),
    ]
    for load in [load_img, load_txt] + small_loads:
        load.start()

    barrier = pltpu.get_barrier_semaphore()
    each(1, n_z, lambda k: pl.semaphore_signal(
        barrier, inc=1, device_id=column(k, 1), device_id_type=MESH))
    each(1, n_plane, lambda k: pl.semaphore_signal(
        barrier, inc=1, device_id=plane(k, 1), device_id_type=MESH))

    def unit_rows(ref):
        wide = ref[...].astype(jnp.float32)
        norm = jnp.sqrt(jnp.sum(wide * wide, axis=-1, keepdims=True) + 1e-06)
        return wide / norm, norm

    for load in small_loads:
        load.wait()
    load_img.wait()
    img_unit, img_norm = unit_rows(img_in)
    sub = lax.broadcasted_iota(jnp.int32, (PAD - rows, width), 0)
    lane = lax.broadcasted_iota(jnp.int32, (PAD - rows, width), 1)
    digits = jnp.zeros((PAD - rows, width), jnp.int32)
    for r in range(rows):
        m = match_ref[r]
        high = m // DIGIT
        digit = jnp.where(sub == 0, high, jnp.where(sub == 1, m - high * DIGIT, 0))
        digits = jnp.where(lane == r, digit, digits)
    img_all[0] = jnp.concatenate([img_unit, digits.astype(jnp.float32)], axis=0).astype(jnp.bfloat16)
    load_txt.wait()
    txt_unit, txt_norm = unit_rows(txt_in)
    txt_all[0] = jnp.concatenate(
        [txt_unit, jnp.zeros((PAD - rows, width), jnp.float32)], axis=0).astype(jnp.bfloat16)

    pl.semaphore_wait(barrier, n_z + n_plane - 2)

    def img_copy(k):
        return pltpu.make_async_remote_copy(
            src_ref=img_all.at[0], dst_ref=img_all.at[k], send_sem=img_out.at[k],
            recv_sem=img_sem.at[k], device_id=plane(k, 1), device_id_type=MESH)

    def txt_copy(k):
        return pltpu.make_async_remote_copy(
            src_ref=txt_all.at[0], dst_ref=txt_all.at[k], send_sem=txt_out.at[k],
            recv_sem=txt_sem.at[k], device_id=column(k, 1), device_id_type=MESH)

    each(1, n_z, lambda k: txt_copy(k).start())
    each(1, n_plane, lambda k: img_copy(k).start())

    each(1, n_z, lambda k: txt_copy(k).wait_recv())
    each(1, n_plane, lambda k: img_copy(k).wait_recv())

    n_rows, n_cols = n_plane * PAD, n_z * PAD
    img_rows = img_all[...].astype(jnp.float32).reshape(n_rows, width).astype(jnp.bfloat16)
    txt_rows = txt_all[...].astype(jnp.float32).reshape(n_cols, width).astype(jnp.bfloat16)
    products = lax.dot_general(
        img_rows, txt_rows, (((1,), (1,)), ((), ())), preferred_element_type=jnp.float32)

    head = img_all[:, :, 0:128].astype(jnp.float32)
    whole = head[:, rows:rows + 1, :] * float(DIGIT) + head[:, rows + 1:rows + 2, :]
    spot = lax.broadcasted_iota(jnp.int32, (n_plane, PAD, 128), 1)
    at = lax.broadcasted_iota(jnp.int32, (n_plane, PAD, 128), 2)
    labels = jnp.sum(
        jnp.where(spot == at, jnp.broadcast_to(whole, (n_plane, PAD, 128)), 0.0),
        axis=-1, keepdims=True).reshape(n_rows, 1)

    row = lax.broadcasted_iota(jnp.int32, (n_rows, n_cols), 0)
    col = lax.broadcasted_iota(jnp.int32, (n_rows, n_cols), 1)
    slot = col // PAD
    place = lax.rem(z - slot + n_z, n_z) * 2 + core
    global_col = (i * n_txt + place) * rows + col % PAD
    valid = (row % PAD < rows) & (col % PAD < rows)
    sign = jnp.where(labels == global_col.astype(jnp.float32), 1.0, -1.0)

    temper = jnp.exp(jnp.full((1, 1), temp_ref[0], jnp.float32))
    scaled = temper * products
    margin = sign * (scaled + bias_ref[0])
    small = jnp.exp(-jnp.abs(margin))
    pair_loss = jnp.maximum(-margin, 0.0) + jnp.log1p(small)
    slopes = jnp.where(valid, -sign * jnp.where(margin >= 0.0, small, 1.0) / (1.0 + small), 0.0)
    pair_loss = jnp.where(valid, pair_loss, 0.0)

    def total(values):
        return jnp.sum(jnp.sum(values, axis=0, keepdims=True), axis=1, keepdims=True)

    lane = lax.broadcasted_iota(jnp.int32, (1, 128), 1)
    sums[0] = jnp.where(
        lane == 0, total(pair_loss),
        jnp.where(lane == 1, total(slopes * scaled), jnp.where(lane == 2, total(slopes), 0.0)))

    def sums_copy(k):
        return pltpu.make_async_remote_copy(
            src_ref=sums.at[0], dst_ref=sums.at[k], send_sem=sums_out.at[k],
            recv_sem=sums_sem.at[k], device_id=plane(k, 1), device_id_type=MESH)

    def col_sums_copy(k):
        return pltpu.make_async_remote_copy(
            src_ref=col_sums.at[0], dst_ref=col_sums.at[k], send_sem=col_sums_out.at[k],
            recv_sem=col_sums_sem.at[k], device_id=column(k, 1), device_id_type=MESH)

    each(1, n_plane, lambda k: sums_copy(k).start())

    weighted = (temper * slopes).astype(jnp.bfloat16)
    txt_term = lax.dot_general(
        weighted, img_rows, (((0,), (0,)), ((), ())), preferred_element_type=jnp.float32)
    txt_part[...] = txt_term.reshape(n_z, PAD, width).astype(jnp.bfloat16)

    def txt_back_copy(k):
        return pltpu.make_async_remote_copy(
            src_ref=txt_part.at[k], dst_ref=txt_back.at[k], send_sem=txt_back_out.at[k],
            recv_sem=txt_back_sem.at[k], device_id=column(k, -1), device_id_type=MESH)

    each(1, n_z, lambda k: txt_back_copy(k).start())

    img_term = jnp.dot(weighted, txt_rows, preferred_element_type=jnp.float32)
    img_part[...] = img_term.reshape(n_plane, PAD, width).astype(jnp.bfloat16)

    def img_back_copy(k):
        return pltpu.make_async_remote_copy(
            src_ref=img_part.at[k], dst_ref=img_back.at[k], send_sem=img_back_out.at[k],
            recv_sem=img_back_sem.at[k], device_id=plane(k, -1), device_id_type=MESH)

    each(1, n_plane, lambda k: img_back_copy(k).start())

    each(1, n_plane, lambda k: sums_copy(k).wait_recv())
    col_sums[0] = jnp.sum(sums[...], axis=0)
    each(1, n_z, lambda k: col_sums_copy(k).start())

    def unit_back(unit, norm, upstream):
        return (upstream - unit * jnp.sum(unit * upstream, axis=-1, keepdims=True)) / norm

    def gather_sum(own, back, n, copy):
        each(1, n, lambda k: copy(k).wait_recv())
        return (own + jnp.sum(back[1:].astype(jnp.float32), axis=0))[0:rows]

    grad_txt_unit = gather_sum(txt_term[0:PAD], txt_back, n_z, txt_back_copy)
    grad_txt_ref[...] = unit_back(txt_unit, txt_norm, grad_txt_unit)
    grad_img_unit = gather_sum(img_term[0:PAD], img_back, n_plane, img_back_copy)
    grad_img_ref[...] = unit_back(img_unit, img_norm, grad_img_unit)

    each(1, n_z, lambda k: col_sums_copy(k).wait_recv())
    batch = jnp.float32(rows * n_img * n_txt)
    totals_ref[...] = jnp.sum(col_sums[...], axis=0) / (batch * batch)

    each(1, n_z, lambda k: (txt_copy(k).wait_send(), txt_back_copy(k).wait_send()))
    each(1, n_plane, lambda k: (img_copy(k).wait_send(), img_back_copy(k).wait_send()))
    each(1, n_z, lambda k: col_sums_copy(k).wait_send())
    each(1, n_plane, lambda k: sums_copy(k).wait_send())


def finish(
    grad_img_ref, grad_txt_ref, totals_ref,
    grad_img_hbm, grad_txt_hbm, loss_hbm, dtemp_hbm, dbias_hbm, loss_ref, dtemp_ref, dbias_ref, sem,
):
    stores = [
        pltpu.make_async_copy(grad_img_ref, grad_img_hbm, sem.at[0]),
        pltpu.make_async_copy(grad_txt_ref, grad_txt_hbm, sem.at[1]),
        pltpu.make_async_copy(loss_ref, loss_hbm, sem.at[2]),
        pltpu.make_async_copy(dtemp_ref, dtemp_hbm, sem.at[3]),
        pltpu.make_async_copy(dbias_ref, dbias_hbm, sem.at[4]),
    ]
    stores[0].start()
    stores[1].start()
    loss_ref[0] = totals_ref[0, 0]
    dtemp_ref[0] = totals_ref[0, 1]
    dbias_ref[0] = totals_ref[0, 2]
    for store in stores[2:]:
        store.start()
    for store in stores:
        store.wait()


def solution(mesh):
    n_img, n_txt = mesh.shape["img"], mesh.shape["txt"]
    n_z, n_plane = n_txt // 2, n_img * 2

    def per_device(img_emb, txt_emb, match, log_temp, bias):
        rows, width = img_emb.shape
        vmem = pl.BlockSpec(memory_space=pltpu.VMEM)
        hbm = pl.BlockSpec(memory_space=pltpu.HBM)
        one = jax.ShapeDtypeStruct((1,), jnp.float32)
        grad = jax.ShapeDtypeStruct((rows, width), jnp.float32)
        dma = pltpu.SemaphoreType.DMA
        parts = pl.pallas_call(
            functools.partial(kernel, n_img, n_txt),
            out_shape=(grad, grad, jax.ShapeDtypeStruct((1, 128), jnp.float32)),
            in_specs=[hbm] * 5,
            out_specs=(vmem,) * 3,
            scratch_shapes=[
                pltpu.VMEM((rows, width), jnp.bfloat16),
                pltpu.VMEM((rows, width), jnp.bfloat16),
                pltpu.SMEM((rows,), jnp.int32),
                pltpu.SMEM((1,), jnp.float32),
                pltpu.SMEM((1,), jnp.float32),
                pltpu.VMEM((n_plane, PAD, width), jnp.bfloat16),
                pltpu.VMEM((n_z, PAD, width), jnp.bfloat16),
                pltpu.VMEM((n_plane, PAD, width), jnp.bfloat16),
                pltpu.VMEM((n_z, PAD, width), jnp.bfloat16),
                pltpu.VMEM((n_plane, PAD, width), jnp.bfloat16),
                pltpu.VMEM((n_z, PAD, width), jnp.bfloat16),
                pltpu.VMEM((n_plane, 1, 128), jnp.float32),
                pltpu.VMEM((n_z, 1, 128), jnp.float32),
                dma((5,)),
            ] + [dma((n_plane,)), dma((n_z,))] * 6,
            compiler_params=pltpu.CompilerParams(
                collective_id=0, has_side_effects=True, vmem_limit_bytes=40 * 1024 * 1024),
        )(img_emb, txt_emb, match, log_temp, bias)
        return pl.pallas_call(
            finish,
            out_shape=(grad, grad, one, one, one),
            in_specs=[vmem] * 3,
            out_specs=(hbm,) * 5,
            scratch_shapes=[pltpu.SMEM((1,), jnp.float32)] * 3 + [dma((5,))],
        )(*parts)

    split = P(("img", "txt"), None)
    return jax.shard_map(
        per_device,
        mesh=mesh,
        in_specs=(split, split, P(("img", "txt")), P(), P()),
        out_specs=(split, split, P(), P(), P()),
        check_vma=False,
    )
```

```python
import functools

import jax
import jax.numpy as jnp
from jax import lax
from jax.experimental import pallas as pl
from jax.experimental.pallas import tpu as pltpu
from jax.sharding import PartitionSpec as P

MESH = pl.DeviceIdType.MESH
PAD = 8
DIGIT = 64


def each(start, stop, body):
    if stop - start <= 32:
        for k in range(start, stop):
            body(k)
    else:
        lax.fori_loop(start, stop, lambda k, c: (body(k), c)[1], 0)


def kernel(
    n_img, n_txt,
    img_hbm, txt_hbm, match_hbm, temp_hbm, bias_hbm,
    grad_img_ref, grad_txt_ref, totals_ref,
    img_in, txt_in, match_ref, temp_ref, bias_ref, img_all, txt_all, img_part, txt_part, img_back, txt_back, sums, col_sums,
    in_sem, img_out, txt_out, img_back_out, txt_back_out, sums_out, col_sums_out,
    img_sem, txt_sem, img_back_sem, txt_back_sem, sums_sem, col_sums_sem,
):
    rows, width = img_in.shape
    n_z = n_txt // 2
    n_plane = n_img * 2
    i = lax.axis_index("img")
    t = lax.axis_index("txt")
    z, core = t // 2, t % 2

    def plane(k, sign):
        return (
            lax.rem(i + sign * (k // 2) + n_img, n_img),
            z * 2 + lax.rem(core + k, 2),
        )

    def column(k, sign):
        return (i, lax.rem(z + sign * k + n_z, n_z) * 2 + core)

    load_img = pltpu.make_async_copy(img_hbm, img_in, in_sem.at[0])
    load_txt = pltpu.make_async_copy(txt_hbm, txt_in, in_sem.at[1])
    small_loads = [
        pltpu.make_async_copy(match_hbm, match_ref, in_sem.at[2]),
        pltpu.make_async_copy(temp_hbm, temp_ref, in_sem.at[3]),
        pltpu.make_async_copy(bias_hbm, bias_ref, in_sem.at[4]),
    ]
    for load in [load_img, load_txt] + small_loads:
        load.start()

    barrier = pltpu.get_barrier_semaphore()
    each(1, n_z, lambda k: pl.semaphore_signal(
        barrier, inc=1, device_id=column(k, 1), device_id_type=MESH))
    each(1, n_plane, lambda k: pl.semaphore_signal(
        barrier, inc=1, device_id=plane(k, 1), device_id_type=MESH))

    def unit_rows(ref):
        wide = ref[...].astype(jnp.float32)
        norm = jnp.sqrt(jnp.sum(wide * wide, axis=-1, keepdims=True) + 1e-06)
        return wide / norm, norm

    for load in small_loads:
        load.wait()
    load_img.wait()
    img_unit, img_norm = unit_rows(img_in)
    sub = lax.broadcasted_iota(jnp.int32, (PAD - rows, width), 0)
    lane = lax.broadcasted_iota(jnp.int32, (PAD - rows, width), 1)
    digits = jnp.zeros((PAD - rows, width), jnp.int32)
    for r in range(rows):
        m = match_ref[r]
        high = m // DIGIT
        digit = jnp.where(sub == 0, high, jnp.where(sub == 1, m - high * DIGIT, 0))
        digits = jnp.where(lane == r, digit, digits)
    img_all[0] = jnp.concatenate([img_unit, digits.astype(jnp.float32)], axis=0).astype(jnp.bfloat16)
    load_txt.wait()
    txt_unit, txt_norm = unit_rows(txt_in)
    txt_all[0] = jnp.concatenate(
        [txt_unit, jnp.zeros((PAD - rows, width), jnp.float32)], axis=0).astype(jnp.bfloat16)

    pl.semaphore_wait(barrier, n_z + n_plane - 2)

    def img_copy(k):
        return pltpu.make_async_remote_copy(
            src_ref=img_all.at[0], dst_ref=img_all.at[k], send_sem=img_out.at[k],
            recv_sem=img_sem.at[k], device_id=plane(k, 1), device_id_type=MESH)

    def txt_copy(k):
        return pltpu.make_async_remote_copy(
            src_ref=txt_all.at[0], dst_ref=txt_all.at[k], send_sem=txt_out.at[k],
            recv_sem=txt_sem.at[k], device_id=column(k, 1), device_id_type=MESH)

    each(1, n_z, lambda k: txt_copy(k).start())
    each(1, n_plane, lambda k: img_copy(k).start())

    each(1, n_z, lambda k: txt_copy(k).wait_recv())
    each(1, n_plane, lambda k: img_copy(k).wait_recv())

    n_rows, n_cols = n_plane * PAD, n_z * PAD
    img_rows = img_all[...].astype(jnp.float32).reshape(n_rows, width).astype(jnp.bfloat16)
    txt_rows = txt_all[...].astype(jnp.float32).reshape(n_cols, width).astype(jnp.bfloat16)
    products = lax.dot_general(
        img_rows, txt_rows, (((1,), (1,)), ((), ())), preferred_element_type=jnp.float32)

    head = img_all[:, :, 0:128].astype(jnp.float32)
    whole = head[:, rows:rows + 1, :] * float(DIGIT) + head[:, rows + 1:rows + 2, :]
    spot = lax.broadcasted_iota(jnp.int32, (n_plane, PAD, 128), 1)
    at = lax.broadcasted_iota(jnp.int32, (n_plane, PAD, 128), 2)
    labels = jnp.sum(
        jnp.where(spot == at, jnp.broadcast_to(whole, (n_plane, PAD, 128)), 0.0),
        axis=-1, keepdims=True).reshape(n_rows, 1)

    row = lax.broadcasted_iota(jnp.int32, (n_rows, n_cols), 0)
    col = lax.broadcasted_iota(jnp.int32, (n_rows, n_cols), 1)
    slot = col // PAD
    place = lax.rem(z - slot + n_z, n_z) * 2 + core
    global_col = (i * n_txt + place) * rows + col % PAD
    valid = (row % PAD < rows) & (col % PAD < rows)
    sign = jnp.where(labels == global_col.astype(jnp.float32), 1.0, -1.0)

    temper = jnp.exp(jnp.full((1, 1), temp_ref[0], jnp.float32))
    scaled = temper * products
    margin = sign * (scaled + bias_ref[0])
    small = jnp.exp(-jnp.abs(margin))
    pair_loss = jnp.maximum(-margin, 0.0) + jnp.log1p(small)
    slopes = jnp.where(valid, -sign * jnp.where(margin >= 0.0, small, 1.0) / (1.0 + small), 0.0)
    pair_loss = jnp.where(valid, pair_loss, 0.0)

    def total(values):
        return jnp.sum(jnp.sum(values, axis=0, keepdims=True), axis=1, keepdims=True)

    lane = lax.broadcasted_iota(jnp.int32, (1, 128), 1)
    sums[0] = jnp.where(
        lane == 0, total(pair_loss),
        jnp.where(lane == 1, total(slopes * scaled), jnp.where(lane == 2, total(slopes), 0.0)))

    def sums_copy(k):
        return pltpu.make_async_remote_copy(
            src_ref=sums.at[0], dst_ref=sums.at[k], send_sem=sums_out.at[k],
            recv_sem=sums_sem.at[k], device_id=plane(k, 1), device_id_type=MESH)

    def col_sums_copy(k):
        return pltpu.make_async_remote_copy(
            src_ref=col_sums.at[0], dst_ref=col_sums.at[k], send_sem=col_sums_out.at[k],
            recv_sem=col_sums_sem.at[k], device_id=column(k, 1), device_id_type=MESH)

    each(1, n_plane, lambda k: sums_copy(k).start())

    weighted = (temper * slopes).astype(jnp.bfloat16)
    txt_term = lax.dot_general(
        weighted, img_rows, (((0,), (0,)), ((), ())), preferred_element_type=jnp.float32)
    txt_part[...] = txt_term.reshape(n_z, PAD, width).astype(jnp.bfloat16)

    def txt_back_copy(k):
        return pltpu.make_async_remote_copy(
            src_ref=txt_part.at[k], dst_ref=txt_back.at[k], send_sem=txt_back_out.at[k],
            recv_sem=txt_back_sem.at[k], device_id=column(k, -1), device_id_type=MESH)

    each(1, n_z, lambda k: txt_back_copy(k).start())

    img_term = jnp.dot(weighted, txt_rows, preferred_element_type=jnp.float32)
    img_part[...] = img_term.reshape(n_plane, PAD, width).astype(jnp.bfloat16)

    def img_back_copy(k):
        return pltpu.make_async_remote_copy(
            src_ref=img_part.at[k], dst_ref=img_back.at[k], send_sem=img_back_out.at[k],
            recv_sem=img_back_sem.at[k], device_id=plane(k, -1), device_id_type=MESH)

    each(1, n_plane, lambda k: img_back_copy(k).start())

    each(1, n_plane, lambda k: sums_copy(k).wait_recv())
    col_sums[0] = jnp.sum(sums[...], axis=0)
    each(1, n_z, lambda k: col_sums_copy(k).start())

    def unit_back(unit, norm, upstream):
        return (upstream - unit * jnp.sum(unit * upstream, axis=-1, keepdims=True)) / norm

    def gather_sum(own, back, n, copy):
        each(1, n, lambda k: copy(k).wait_recv())
        return (own + jnp.sum(back[1:].astype(jnp.float32), axis=0))[0:rows]

    grad_txt_unit = gather_sum(txt_term[0:PAD], txt_back, n_z, txt_back_copy)
    grad_txt_ref[...] = unit_back(txt_unit, txt_norm, grad_txt_unit)
    grad_img_unit = gather_sum(img_term[0:PAD], img_back, n_plane, img_back_copy)
    grad_img_ref[...] = unit_back(img_unit, img_norm, grad_img_unit)

    each(1, n_z, lambda k: col_sums_copy(k).wait_recv())
    batch = jnp.float32(rows * n_img * n_txt)
    totals_ref[...] = jnp.sum(col_sums[...], axis=0) / (batch * batch)

    each(1, n_z, lambda k: (txt_copy(k).wait_send(), txt_back_copy(k).wait_send()))
    each(1, n_plane, lambda k: (img_copy(k).wait_send(), img_back_copy(k).wait_send()))
    each(1, n_z, lambda k: col_sums_copy(k).wait_send())
    each(1, n_plane, lambda k: sums_copy(k).wait_send())


def finish(
    grad_img_ref, grad_txt_ref, totals_ref,
    grad_img_hbm, grad_txt_hbm, loss_hbm, dtemp_hbm, dbias_hbm, loss_ref, dtemp_ref, dbias_ref, sem,
):
    stores = [
        pltpu.make_async_copy(grad_img_ref, grad_img_hbm, sem.at[0]),
        pltpu.make_async_copy(grad_txt_ref, grad_txt_hbm, sem.at[1]),
        pltpu.make_async_copy(loss_ref, loss_hbm, sem.at[2]),
        pltpu.make_async_copy(dtemp_ref, dtemp_hbm, sem.at[3]),
        pltpu.make_async_copy(dbias_ref, dbias_hbm, sem.at[4]),
    ]
    stores[0].start()
    stores[1].start()
    loss_ref[0] = totals_ref[0, 0]
    dtemp_ref[0] = totals_ref[0, 1]
    dbias_ref[0] = totals_ref[0, 2]
    for store in stores[2:]:
        store.start()
    for store in stores:
        store.wait()


def solution(mesh):
    n_img, n_txt = mesh.shape["img"], mesh.shape["txt"]
    n_z, n_plane = n_txt // 2, n_img * 2

    def per_device(img_emb, txt_emb, match, log_temp, bias):
        rows, width = img_emb.shape
        vmem = pl.BlockSpec(memory_space=pltpu.VMEM)
        hbm = pl.BlockSpec(memory_space=pltpu.HBM)
        one = jax.ShapeDtypeStruct((1,), jnp.float32)
        grad = jax.ShapeDtypeStruct((rows, width), jnp.float32)
        dma = pltpu.SemaphoreType.DMA
        img_emb, txt_emb, match = (
            pltpu.with_memory_space_constraint(x, pltpu.HBM) for x in (img_emb, txt_emb, match))
        parts = pl.pallas_call(
            functools.partial(kernel, n_img, n_txt),
            out_shape=(pltpu.VMEM((rows, width), jnp.float32),) * 2 + (pltpu.VMEM((1, 128), jnp.float32),),
            in_specs=[hbm] * 5,
            out_specs=(vmem,) * 3,
            scratch_shapes=[
                pltpu.VMEM((rows, width), jnp.bfloat16),
                pltpu.VMEM((rows, width), jnp.bfloat16),
                pltpu.SMEM((rows,), jnp.int32),
                pltpu.SMEM((1,), jnp.float32),
                pltpu.SMEM((1,), jnp.float32),
                pltpu.VMEM((n_plane, PAD, width), jnp.bfloat16),
                pltpu.VMEM((n_z, PAD, width), jnp.bfloat16),
                pltpu.VMEM((n_plane, PAD, width), jnp.bfloat16),
                pltpu.VMEM((n_z, PAD, width), jnp.bfloat16),
                pltpu.VMEM((n_plane, PAD, width), jnp.bfloat16),
                pltpu.VMEM((n_z, PAD, width), jnp.bfloat16),
                pltpu.VMEM((n_plane, 1, 128), jnp.float32),
                pltpu.VMEM((n_z, 1, 128), jnp.float32),
                dma((5,)),
            ] + [dma((n_plane,)), dma((n_z,))] * 6,
            compiler_params=pltpu.CompilerParams(
                collective_id=0, has_side_effects=True, vmem_limit_bytes=40 * 1024 * 1024),
        )(img_emb, txt_emb, match, log_temp, bias)
        return pl.pallas_call(
            finish,
            out_shape=(grad, grad, one, one, one),
            in_specs=[vmem] * 3,
            out_specs=(hbm,) * 5,
            scratch_shapes=[pltpu.SMEM((1,), jnp.float32)] * 3 + [dma((5,))],
        )(*parts)

    split = P(("img", "txt"), None)
    return jax.shard_map(
        per_device,
        mesh=mesh,
        in_specs=(split, split, P(("img", "txt")), P(), P()),
        out_specs=(split, split, P(), P(), P()),
        check_vma=False,
    )
```

```python
import functools

import jax
import jax.numpy as jnp
from jax import lax
from jax.experimental import pallas as pl
from jax.experimental.pallas import tpu as pltpu
from jax.sharding import PartitionSpec as P

MESH = pl.DeviceIdType.MESH
PAD = 8
DIGIT = 64


def each(start, stop, body):
    if stop - start <= 32:
        for k in range(start, stop):
            body(k)
    else:
        lax.fori_loop(start, stop, lambda k, c: (body(k), c)[1], 0)


def kernel(
    n_img, n_txt,
    img_hbm, txt_hbm, match_hbm, temp_hbm, bias_hbm,
    grad_img_ref, grad_txt_ref, totals_ref,
    img_in, txt_in, match_ref, temp_ref, bias_ref, img_all, txt_all, img_part, txt_part, img_back, txt_back, sums, col_sums,
    in_sem, img_out, txt_out, img_back_out, txt_back_out, sums_out, col_sums_out,
    img_sem, txt_sem, img_back_sem, txt_back_sem, sums_sem, col_sums_sem,
):
    rows, width = img_in.shape
    n_z = n_txt // 2
    n_plane = n_img * 2
    i = lax.axis_index("img")
    t = lax.axis_index("txt")
    z, core = t // 2, t % 2

    def plane(k, sign):
        return (
            lax.rem(i + sign * (k // 2) + n_img, n_img),
            z * 2 + lax.rem(core + k, 2),
        )

    def column(k, sign):
        return (i, lax.rem(z + sign * k + n_z, n_z) * 2 + core)

    def anyone(k):
        other = lax.rem(i * n_txt + t + k, n_img * n_txt)
        return (other // n_txt, lax.rem(other, n_txt))

    load_img = pltpu.make_async_copy(img_hbm, img_in, in_sem.at[0])
    load_txt = pltpu.make_async_copy(txt_hbm, txt_in, in_sem.at[1])
    small_loads = [
        pltpu.make_async_copy(match_hbm, match_ref, in_sem.at[2]),
        pltpu.make_async_copy(temp_hbm, temp_ref, in_sem.at[3]),
        pltpu.make_async_copy(bias_hbm, bias_ref, in_sem.at[4]),
    ]
    for load in [load_img, load_txt] + small_loads:
        load.start()

    barrier = pltpu.get_barrier_semaphore()
    each(1, n_img * n_txt, lambda k: pl.semaphore_signal(
        barrier, inc=1, device_id=anyone(k), device_id_type=MESH))

    def unit_rows(ref):
        wide = ref[...].astype(jnp.float32)
        norm = jnp.sqrt(jnp.sum(wide * wide, axis=-1, keepdims=True) + 1e-06)
        return wide / norm, norm

    for load in small_loads:
        load.wait()
    load_img.wait()
    img_unit, img_norm = unit_rows(img_in)
    sub = lax.broadcasted_iota(jnp.int32, (PAD - rows, width), 0)
    lane = lax.broadcasted_iota(jnp.int32, (PAD - rows, width), 1)
    digits = jnp.zeros((PAD - rows, width), jnp.int32)
    for r in range(rows):
        m = match_ref[r]
        high = m // DIGIT
        digit = jnp.where(sub == 0, high, jnp.where(sub == 1, m - high * DIGIT, 0))
        digits = jnp.where(lane == r, digit, digits)
    img_all[0] = jnp.concatenate([img_unit, digits.astype(jnp.float32)], axis=0).astype(jnp.bfloat16)
    load_txt.wait()
    txt_unit, txt_norm = unit_rows(txt_in)
    txt_all[0] = jnp.concatenate(
        [txt_unit, jnp.zeros((PAD - rows, width), jnp.float32)], axis=0).astype(jnp.bfloat16)

    pl.semaphore_wait(barrier, n_img * n_txt - 1)

    def img_copy(k):
        return pltpu.make_async_remote_copy(
            src_ref=img_all.at[0], dst_ref=img_all.at[k], send_sem=img_out.at[k],
            recv_sem=img_sem.at[k], device_id=plane(k, 1), device_id_type=MESH)

    def txt_copy(k):
        return pltpu.make_async_remote_copy(
            src_ref=txt_all.at[0], dst_ref=txt_all.at[k], send_sem=txt_out.at[k],
            recv_sem=txt_sem.at[k], device_id=column(k, 1), device_id_type=MESH)

    each(1, n_z, lambda k: txt_copy(k).start())
    each(1, n_plane, lambda k: img_copy(k).start())

    each(1, n_z, lambda k: txt_copy(k).wait_recv())
    each(1, n_plane, lambda k: img_copy(k).wait_recv())

    n_rows, n_cols = n_plane * PAD, n_z * PAD
    img_rows = img_all[...].astype(jnp.float32).reshape(n_rows, width).astype(jnp.bfloat16)
    txt_rows = txt_all[...].astype(jnp.float32).reshape(n_cols, width).astype(jnp.bfloat16)
    products = lax.dot_general(
        img_rows, txt_rows, (((1,), (1,)), ((), ())), preferred_element_type=jnp.float32)

    head = img_all[:, :, 0:128].astype(jnp.float32)
    whole = head[:, rows:rows + 1, :] * float(DIGIT) + head[:, rows + 1:rows + 2, :]
    spot = lax.broadcasted_iota(jnp.int32, (n_plane, PAD, 128), 1)
    at = lax.broadcasted_iota(jnp.int32, (n_plane, PAD, 128), 2)
    labels = jnp.sum(
        jnp.where(spot == at, jnp.broadcast_to(whole, (n_plane, PAD, 128)), 0.0),
        axis=-1, keepdims=True).reshape(n_rows, 1)

    row = lax.broadcasted_iota(jnp.int32, (n_rows, n_cols), 0)
    col = lax.broadcasted_iota(jnp.int32, (n_rows, n_cols), 1)
    slot = col // PAD
    place = lax.rem(z - slot + n_z, n_z) * 2 + core
    global_col = (i * n_txt + place) * rows + col % PAD
    valid = (row % PAD < rows) & (col % PAD < rows)
    sign = jnp.where(labels == global_col.astype(jnp.float32), 1.0, -1.0)

    temper = jnp.exp(jnp.full((1, 1), temp_ref[0], jnp.float32))
    scaled = temper * products
    margin = sign * (scaled + bias_ref[0])
    small = jnp.exp(-jnp.abs(margin))
    pair_loss = jnp.maximum(-margin, 0.0) + jnp.log1p(small)
    slopes = jnp.where(valid, -sign * jnp.where(margin >= 0.0, small, 1.0) / (1.0 + small), 0.0)
    pair_loss = jnp.where(valid, pair_loss, 0.0)

    def total(values):
        return jnp.sum(jnp.sum(values, axis=0, keepdims=True), axis=1, keepdims=True)

    lane = lax.broadcasted_iota(jnp.int32, (1, 128), 1)
    sums[0] = jnp.where(
        lane == 0, total(pair_loss),
        jnp.where(lane == 1, total(slopes * scaled), jnp.where(lane == 2, total(slopes), 0.0)))

    def sums_copy(k):
        return pltpu.make_async_remote_copy(
            src_ref=sums.at[0], dst_ref=sums.at[k], send_sem=sums_out.at[k],
            recv_sem=sums_sem.at[k], device_id=anyone(k), device_id_type=MESH)

    def col_sums_copy(k):
        return pltpu.make_async_remote_copy(
            src_ref=col_sums.at[0], dst_ref=col_sums.at[k], send_sem=col_sums_out.at[k],
            recv_sem=col_sums_sem.at[k], device_id=column(k, 1), device_id_type=MESH)

    each(1, n_img * n_txt, lambda k: sums_copy(k).start())

    weighted = (temper * slopes).astype(jnp.bfloat16)
    txt_term = lax.dot_general(
        weighted, img_rows, (((0,), (0,)), ((), ())), preferred_element_type=jnp.float32)
    txt_part[...] = txt_term.reshape(n_z, PAD, width).astype(jnp.bfloat16)

    def txt_back_copy(k):
        return pltpu.make_async_remote_copy(
            src_ref=txt_part.at[k], dst_ref=txt_back.at[k], send_sem=txt_back_out.at[k],
            recv_sem=txt_back_sem.at[k], device_id=column(k, -1), device_id_type=MESH)

    each(1, n_z, lambda k: txt_back_copy(k).start())

    img_term = jnp.dot(weighted, txt_rows, preferred_element_type=jnp.float32)
    img_part[...] = img_term.reshape(n_plane, PAD, width).astype(jnp.bfloat16)

    def img_back_copy(k):
        return pltpu.make_async_remote_copy(
            src_ref=img_part.at[k], dst_ref=img_back.at[k], send_sem=img_back_out.at[k],
            recv_sem=img_back_sem.at[k], device_id=plane(k, -1), device_id_type=MESH)

    each(1, n_plane, lambda k: img_back_copy(k).start())


    def unit_back(unit, norm, upstream):
        return (upstream - unit * jnp.sum(unit * upstream, axis=-1, keepdims=True)) / norm

    def gather_sum(own, back, n, copy):
        each(1, n, lambda k: copy(k).wait_recv())
        return (own + jnp.sum(back[1:].astype(jnp.float32), axis=0))[0:rows]

    grad_txt_unit = gather_sum(txt_term[0:PAD], txt_back, n_z, txt_back_copy)
    grad_txt_ref[...] = unit_back(txt_unit, txt_norm, grad_txt_unit)
    grad_img_unit = gather_sum(img_term[0:PAD], img_back, n_plane, img_back_copy)
    grad_img_ref[...] = unit_back(img_unit, img_norm, grad_img_unit)

    each(1, n_img * n_txt, lambda k: sums_copy(k).wait_recv())
    batch = jnp.float32(rows * n_img * n_txt)
    totals_ref[...] = jnp.sum(sums[...], axis=0) / (batch * batch)

    each(1, n_z, lambda k: (txt_copy(k).wait_send(), txt_back_copy(k).wait_send()))
    each(1, n_plane, lambda k: (img_copy(k).wait_send(), img_back_copy(k).wait_send()))
    each(1, n_img * n_txt, lambda k: sums_copy(k).wait_send())


def finish(
    grad_img_ref, grad_txt_ref, totals_ref,
    grad_img_hbm, grad_txt_hbm, loss_hbm, dtemp_hbm, dbias_hbm, loss_ref, dtemp_ref, dbias_ref, sem,
):
    stores = [
        pltpu.make_async_copy(grad_img_ref, grad_img_hbm, sem.at[0]),
        pltpu.make_async_copy(grad_txt_ref, grad_txt_hbm, sem.at[1]),
        pltpu.make_async_copy(loss_ref, loss_hbm, sem.at[2]),
        pltpu.make_async_copy(dtemp_ref, dtemp_hbm, sem.at[3]),
        pltpu.make_async_copy(dbias_ref, dbias_hbm, sem.at[4]),
    ]
    stores[0].start()
    stores[1].start()
    loss_ref[0] = totals_ref[0, 0]
    dtemp_ref[0] = totals_ref[0, 1]
    dbias_ref[0] = totals_ref[0, 2]
    for store in stores[2:]:
        store.start()
    for store in stores:
        store.wait()


def solution(mesh):
    n_img, n_txt = mesh.shape["img"], mesh.shape["txt"]
    n_z, n_plane = n_txt // 2, n_img * 2

    def per_device(img_emb, txt_emb, match, log_temp, bias):
        rows, width = img_emb.shape
        vmem = pl.BlockSpec(memory_space=pltpu.VMEM)
        hbm = pl.BlockSpec(memory_space=pltpu.HBM)
        one = jax.ShapeDtypeStruct((1,), jnp.float32)
        grad = jax.ShapeDtypeStruct((rows, width), jnp.float32)
        dma = pltpu.SemaphoreType.DMA
        img_emb, txt_emb, match = (
            pltpu.with_memory_space_constraint(x, pltpu.HBM) for x in (img_emb, txt_emb, match))
        parts = pl.pallas_call(
            functools.partial(kernel, n_img, n_txt),
            out_shape=(pltpu.VMEM((rows, width), jnp.float32),) * 2 + (pltpu.VMEM((1, 128), jnp.float32),),
            in_specs=[hbm] * 5,
            out_specs=(vmem,) * 3,
            scratch_shapes=[
                pltpu.VMEM((rows, width), jnp.bfloat16),
                pltpu.VMEM((rows, width), jnp.bfloat16),
                pltpu.SMEM((rows,), jnp.int32),
                pltpu.SMEM((1,), jnp.float32),
                pltpu.SMEM((1,), jnp.float32),
                pltpu.VMEM((n_plane, PAD, width), jnp.bfloat16),
                pltpu.VMEM((n_z, PAD, width), jnp.bfloat16),
                pltpu.VMEM((n_plane, PAD, width), jnp.bfloat16),
                pltpu.VMEM((n_z, PAD, width), jnp.bfloat16),
                pltpu.VMEM((n_plane, PAD, width), jnp.bfloat16),
                pltpu.VMEM((n_z, PAD, width), jnp.bfloat16),
                pltpu.VMEM((n_img * n_txt, 1, 128), jnp.float32),
                pltpu.VMEM((n_z, 1, 128), jnp.float32),
                dma((5,)),
            ] + ([dma((n_plane,)), dma((n_z,))] * 2 + [dma((n_img * n_txt,)), dma((n_z,))]) * 2,
            compiler_params=pltpu.CompilerParams(
                collective_id=0, has_side_effects=True, vmem_limit_bytes=16 * 1024 * 1024),
        )(img_emb, txt_emb, match, log_temp, bias)
        return pl.pallas_call(
            finish,
            out_shape=(grad, grad, one, one, one),
            compiler_params=pltpu.CompilerParams(vmem_limit_bytes=4 * 1024 * 1024),
            in_specs=[vmem] * 3,
            out_specs=(hbm,) * 5,
            scratch_shapes=[pltpu.SMEM((1,), jnp.float32)] * 3 + [dma((5,))],
        )(*parts)

    split = P(("img", "txt"), None)
    return jax.shard_map(
        per_device,
        mesh=mesh,
        in_specs=(split, split, P(("img", "txt")), P(), P()),
        out_specs=(split, split, P(), P(), P()),
        check_vma=False,
    )
```

```python
import functools

import jax
import jax.numpy as jnp
from jax import lax
from jax.experimental import pallas as pl
from jax.experimental.pallas import tpu as pltpu
from jax.sharding import PartitionSpec as P

MESH = pl.DeviceIdType.MESH
PAD = 8
DIGIT = 64


def each(start, stop, body):
    if stop - start <= 32:
        for k in range(start, stop):
            body(k)
    else:
        lax.fori_loop(start, stop, lambda k, c: (body(k), c)[1], 0)


def kernel(
    n_img, n_txt,
    img_hbm, txt_hbm, match_hbm, temp_hbm, bias_hbm,
    grad_img_ref, grad_txt_ref, totals_ref,
    img_in, txt_in, match_ref, temp_ref, bias_ref, img_all, txt_all, img_part, txt_part, img_back, txt_back, sums,
    in_sem, img_out, txt_out, img_back_out, txt_back_out, sums_out,
    img_sem, txt_sem, img_back_sem, txt_back_sem, sums_sem,
):
    rows, width = img_in.shape
    n_z = n_txt // 2
    n_plane = n_img * 2
    i = lax.axis_index("img")
    t = lax.axis_index("txt")
    z, core = t // 2, t % 2

    def wrap(value, n):
        return jnp.where(value >= n, value - n, value)

    def shift(value, k, sign, n):
        return wrap(value + k, n) if sign > 0 else wrap(value + (n - k), n)

    def plane(k, sign):
        flip = k % 2
        return (shift(i, k // 2, sign, n_img), z * 2 + core + flip * (1 - 2 * core))

    def column(k, sign):
        return (i, shift(z, k, sign, n_z) * 2 + core)

    def anyone(k):
        return (shift(i, k // n_txt, 1, n_img), shift(t, k % n_txt, 1, n_txt))

    def wait_all(ref, n, sem):
        slots = ref.at[pl.ds(1, n - 1)]
        pltpu.make_async_copy(slots, slots, sem.at[0]).wait()

    load_img = pltpu.make_async_copy(img_hbm, img_in, in_sem.at[0])
    load_txt = pltpu.make_async_copy(txt_hbm, txt_in, in_sem.at[1])
    small_loads = [
        pltpu.make_async_copy(match_hbm, match_ref, in_sem.at[2]),
        pltpu.make_async_copy(temp_hbm, temp_ref, in_sem.at[3]),
        pltpu.make_async_copy(bias_hbm, bias_ref, in_sem.at[4]),
    ]
    for load in [load_img, load_txt] + small_loads:
        load.start()

    barrier = pltpu.get_barrier_semaphore()
    each(1, n_img * n_txt, lambda k: pl.semaphore_signal(
        barrier, inc=1, device_id=anyone(k), device_id_type=MESH))

    def unit_rows(ref):
        wide = ref[...].astype(jnp.float32)
        norm = jnp.sqrt(jnp.sum(wide * wide, axis=-1, keepdims=True) + 1e-06)
        return wide / norm, norm

    for load in small_loads:
        load.wait()
    load_img.wait()
    img_unit, img_norm = unit_rows(img_in)
    sub = lax.broadcasted_iota(jnp.int32, (PAD - rows, width), 0)
    lane = lax.broadcasted_iota(jnp.int32, (PAD - rows, width), 1)
    digits = jnp.zeros((PAD - rows, width), jnp.int32)
    for r in range(rows):
        m = match_ref[r]
        high = m // DIGIT
        digit = jnp.where(sub == 0, high, jnp.where(sub == 1, m - high * DIGIT, 0))
        digits = jnp.where(lane == r, digit, digits)
    img_all[0] = jnp.concatenate([img_unit, digits.astype(jnp.float32)], axis=0).astype(jnp.bfloat16)
    load_txt.wait()
    txt_unit, txt_norm = unit_rows(txt_in)
    txt_all[0] = jnp.concatenate(
        [txt_unit, jnp.zeros((PAD - rows, width), jnp.float32)], axis=0).astype(jnp.bfloat16)

    pl.semaphore_wait(barrier, n_img * n_txt - 1)

    def img_copy(k):
        return pltpu.make_async_remote_copy(
            src_ref=img_all.at[0], dst_ref=img_all.at[k], send_sem=img_out.at[0],
            recv_sem=img_sem.at[0], device_id=plane(k, 1), device_id_type=MESH)

    def txt_copy(k):
        return pltpu.make_async_remote_copy(
            src_ref=txt_all.at[0], dst_ref=txt_all.at[k], send_sem=txt_out.at[0],
            recv_sem=txt_sem.at[0], device_id=column(k, 1), device_id_type=MESH)

    each(1, n_z, lambda k: txt_copy(k).start())
    each(1, n_plane, lambda k: img_copy(k).start())

    wait_all(txt_all, n_z, txt_sem)
    wait_all(img_all, n_plane, img_sem)

    n_rows, n_cols = n_plane * PAD, n_z * PAD
    img_rows = img_all[...].astype(jnp.float32).reshape(n_rows, width).astype(jnp.bfloat16)
    txt_rows = txt_all[...].astype(jnp.float32).reshape(n_cols, width).astype(jnp.bfloat16)
    products = lax.dot_general(
        img_rows, txt_rows, (((1,), (1,)), ((), ())), preferred_element_type=jnp.float32)

    head = img_all[:, :, 0:128].astype(jnp.float32)
    whole = head[:, rows:rows + 1, :] * float(DIGIT) + head[:, rows + 1:rows + 2, :]
    spot = lax.broadcasted_iota(jnp.int32, (n_plane, PAD, 128), 1)
    at = lax.broadcasted_iota(jnp.int32, (n_plane, PAD, 128), 2)
    labels = jnp.sum(
        jnp.where(spot == at, jnp.broadcast_to(whole, (n_plane, PAD, 128)), 0.0),
        axis=-1, keepdims=True).reshape(n_rows, 1)

    row = lax.broadcasted_iota(jnp.int32, (n_rows, n_cols), 0)
    col = lax.broadcasted_iota(jnp.int32, (n_rows, n_cols), 1)
    slot = col // PAD
    place = lax.rem(z - slot + n_z, n_z) * 2 + core
    global_col = (i * n_txt + place) * rows + col % PAD
    valid = (row % PAD < rows) & (col % PAD < rows)
    sign = jnp.where(labels == global_col.astype(jnp.float32), 1.0, -1.0)

    temper = jnp.exp(jnp.full((1, 1), temp_ref[0], jnp.float32))
    scaled = temper * products
    margin = sign * (scaled + bias_ref[0])
    small = jnp.exp(-jnp.abs(margin))
    pair_loss = jnp.maximum(-margin, 0.0) + jnp.log1p(small)
    slopes = jnp.where(valid, -sign * jnp.where(margin >= 0.0, small, 1.0) / (1.0 + small), 0.0)
    pair_loss = jnp.where(valid, pair_loss, 0.0)

    def total(values):
        return jnp.sum(jnp.sum(values, axis=0, keepdims=True), axis=1, keepdims=True)

    lane = lax.broadcasted_iota(jnp.int32, (1, 128), 1)
    sums[0] = jnp.where(
        lane == 0, total(pair_loss),
        jnp.where(lane == 1, total(slopes * scaled), jnp.where(lane == 2, total(slopes), 0.0)))

    def sums_copy(k):
        return pltpu.make_async_remote_copy(
            src_ref=sums.at[0], dst_ref=sums.at[k], send_sem=sums_out.at[0],
            recv_sem=sums_sem.at[0], device_id=anyone(k), device_id_type=MESH)

    each(1, n_img * n_txt, lambda k: sums_copy(k).start())

    weighted = (temper * slopes).astype(jnp.bfloat16)
    txt_term = lax.dot_general(
        weighted, img_rows, (((0,), (0,)), ((), ())), preferred_element_type=jnp.float32)
    txt_part[...] = txt_term.reshape(n_z, PAD, width).astype(jnp.bfloat16)

    def txt_back_copy(k):
        return pltpu.make_async_remote_copy(
            src_ref=txt_part.at[k], dst_ref=txt_back.at[k], send_sem=txt_back_out.at[0],
            recv_sem=txt_back_sem.at[0], device_id=column(k, -1), device_id_type=MESH)

    each(1, n_z, lambda k: txt_back_copy(k).start())

    img_term = jnp.dot(weighted, txt_rows, preferred_element_type=jnp.float32)
    img_part[...] = img_term.reshape(n_plane, PAD, width).astype(jnp.bfloat16)

    def img_back_copy(k):
        return pltpu.make_async_remote_copy(
            src_ref=img_part.at[k], dst_ref=img_back.at[k], send_sem=img_back_out.at[0],
            recv_sem=img_back_sem.at[0], device_id=plane(k, -1), device_id_type=MESH)

    each(1, n_plane, lambda k: img_back_copy(k).start())


    def unit_back(unit, norm, upstream):
        return (upstream - unit * jnp.sum(unit * upstream, axis=-1, keepdims=True)) / norm

    def gather_sum(own, back, n, sem):
        wait_all(back, n, sem)
        return (own + jnp.sum(back[1:].astype(jnp.float32), axis=0))[0:rows]

    grad_txt_unit = gather_sum(txt_term[0:PAD], txt_back, n_z, txt_back_sem)
    grad_txt_ref[...] = unit_back(txt_unit, txt_norm, grad_txt_unit)
    grad_img_unit = gather_sum(img_term[0:PAD], img_back, n_plane, img_back_sem)
    grad_img_ref[...] = unit_back(img_unit, img_norm, grad_img_unit)

    wait_all(sums, n_img * n_txt, sums_sem)
    batch = jnp.float32(rows * n_img * n_txt)
    totals_ref[...] = jnp.sum(sums[...], axis=0) / (batch * batch)

    wait_all(txt_all, n_z, txt_out)
    wait_all(img_all, n_plane, img_out)
    wait_all(txt_back, n_z, txt_back_out)
    wait_all(img_back, n_plane, img_back_out)
    wait_all(sums, n_img * n_txt, sums_out)


def finish(
    grad_img_ref, grad_txt_ref, totals_ref,
    grad_img_hbm, grad_txt_hbm, loss_hbm, dtemp_hbm, dbias_hbm, loss_ref, dtemp_ref, dbias_ref, sem,
):
    stores = [
        pltpu.make_async_copy(grad_img_ref, grad_img_hbm, sem.at[0]),
        pltpu.make_async_copy(grad_txt_ref, grad_txt_hbm, sem.at[1]),
        pltpu.make_async_copy(loss_ref, loss_hbm, sem.at[2]),
        pltpu.make_async_copy(dtemp_ref, dtemp_hbm, sem.at[3]),
        pltpu.make_async_copy(dbias_ref, dbias_hbm, sem.at[4]),
    ]
    stores[0].start()
    stores[1].start()
    loss_ref[0] = totals_ref[0, 0]
    dtemp_ref[0] = totals_ref[0, 1]
    dbias_ref[0] = totals_ref[0, 2]
    for store in stores[2:]:
        store.start()
    for store in stores:
        store.wait()


def solution(mesh):
    n_img, n_txt = mesh.shape["img"], mesh.shape["txt"]
    n_z, n_plane = n_txt // 2, n_img * 2

    def per_device(img_emb, txt_emb, match, log_temp, bias):
        rows, width = img_emb.shape
        vmem = pl.BlockSpec(memory_space=pltpu.VMEM)
        hbm = pl.BlockSpec(memory_space=pltpu.HBM)
        one = jax.ShapeDtypeStruct((1,), jnp.float32)
        grad = jax.ShapeDtypeStruct((rows, width), jnp.float32)
        dma = pltpu.SemaphoreType.DMA
        img_emb, txt_emb, match = (
            pltpu.with_memory_space_constraint(x, pltpu.HBM) for x in (img_emb, txt_emb, match))
        parts = pl.pallas_call(
            functools.partial(kernel, n_img, n_txt),
            out_shape=(pltpu.VMEM((rows, width), jnp.float32),) * 2 + (pltpu.VMEM((1, 128), jnp.float32),),
            in_specs=[hbm] * 5,
            out_specs=(vmem,) * 3,
            scratch_shapes=[
                pltpu.VMEM((rows, width), jnp.bfloat16),
                pltpu.VMEM((rows, width), jnp.bfloat16),
                pltpu.SMEM((rows,), jnp.int32),
                pltpu.SMEM((1,), jnp.float32),
                pltpu.SMEM((1,), jnp.float32),
                pltpu.VMEM((n_plane, PAD, width), jnp.bfloat16),
                pltpu.VMEM((n_z, PAD, width), jnp.bfloat16),
                pltpu.VMEM((n_plane, PAD, width), jnp.bfloat16),
                pltpu.VMEM((n_z, PAD, width), jnp.bfloat16),
                pltpu.VMEM((n_plane, PAD, width), jnp.bfloat16),
                pltpu.VMEM((n_z, PAD, width), jnp.bfloat16),
                pltpu.VMEM((n_img * n_txt, 1, 128), jnp.float32),
                dma((5,)),
            ] + [dma((1,))] * 10,
            compiler_params=pltpu.CompilerParams(
                collective_id=0, has_side_effects=True, vmem_limit_bytes=16 * 1024 * 1024),
        )(img_emb, txt_emb, match, log_temp, bias)
        return pl.pallas_call(
            finish,
            out_shape=(grad, grad, one, one, one),
            compiler_params=pltpu.CompilerParams(vmem_limit_bytes=4 * 1024 * 1024),
            in_specs=[vmem] * 3,
            out_specs=(hbm,) * 5,
            scratch_shapes=[pltpu.SMEM((1,), jnp.float32)] * 3 + [dma((5,))],
        )(*parts)

    split = P(("img", "txt"), None)
    return jax.shard_map(
        per_device,
        mesh=mesh,
        in_specs=(split, split, P(("img", "txt")), P(), P()),
        out_specs=(split, split, P(), P(), P()),
        check_vma=False,
    )
```
